32 devices in a mesh: row: 8 (over z, y), col: 4 (over x, core).
Axes of the slice: x: 2, y: 2, z: 4, core: 2. Of those that a mesh axis runs over, the one named last changes fastest.
Arguments:
- archive: float32 [32768, 256], P('row'), may hold values from -6 to 6
- slab_index: int32 [12288], replicated, may hold values from 0 to 32767
- targets: float32 [12288, 256], P('col'), may hold values from -6 to 6
Outputs:
- panels: float32 [12288, 512], P('row')
- applied: float32 [12288, 256], P(('row', 'col'))
The draws below stay inside these ranges and needn't reach their ends.
Inputs may be any that keep to these rules, and one draw needn't show every extreme that they name: `slab_index`: values may repeat.
All inputs are finite; a program needn't handle non-finite values.
Results may differ from the reference program's by a relative error of at most 0.0003.
Values sent between devices are 32-bit elements; how exact they have to be, the bound alone decides.
A program may use at most 128 MiB of HBM per device.

```python
import jax
import jax.numpy as jnp
from jax import lax

F = 256
ORDER = 12288
NB = 256
PANELS = 2
NT = 256
ARCHIVE = 32768
N_ROW = 8
N_COL = 4


def place_ends(array, own_key, low, high):
    dims = array.shape
    spot = [jax.random.randint(jax.random.fold_in(own_key, axis), (), 0, dims[axis]) for axis in range(len(dims))]
    array = array.at[tuple(spot)].set(low)
    longest = dims.index(max(dims))
    spot[longest] = (spot[longest] + 1) % dims[longest]
    return array.at[tuple(spot)].set(high)


def level_of(own_key, extent, split, low, top_value):
    level, own = 1.0, jax.random.fold_in(own_key, 6)
    for position, blocks in split:
        heights = jnp.exp(jax.random.uniform(jax.random.fold_in(own, position), (blocks,), jnp.float32, low / len(split), top_value / len(split)))
        level = level * jnp.repeat(heights, extent[position] // blocks).reshape([-1 if axis == position else 1 for axis in range(len(extent))])
    return level


def bell_draw(stream_key, extent, spread, bound, pieces=(), kind=jnp.bfloat16):
    drawn = jax.random.normal(stream_key, extent, jnp.float32) * spread
    if len(pieces) > 0:
        drawn = level_of(stream_key, extent, pieces, -0.22, 0.18) * drawn
    return jnp.clip(drawn, min=-bound, max=bound).astype(kind)


def setup_inputs(seed: int = 0) -> dict:
    arg_keys = jax.random.split(jax.random.key(seed), 4)
    return {
        "archive": bell_draw(arg_keys[0], (ARCHIVE, F), 1.0, 6.0, ((0, 8),), jnp.float32),
        "slab_index": place_ends(jax.random.randint(arg_keys[1], (ORDER,), 0, ARCHIVE), jax.random.fold_in(arg_keys[1], 1), 0, ARCHIVE - 1).astype(jnp.int32),
        "targets": bell_draw(arg_keys[2], (ORDER, NT), 1.0, 6.0, ((0, 4),), jnp.float32),
    }


precise = lax.Precision.HIGHEST
length_scale = 16.0
nugget = 1.0
root_five = 5.0 ** 0.5

def matern(left, right, left_ids, right_ids):
    left_sq = lax.optimization_barrier(jnp.sum(left * left, axis=1))
    right_sq = lax.optimization_barrier(jnp.sum(right * right, axis=1))
    cross = lax.dot_general(left.astype(jnp.float32), right.astype(jnp.float32), (((1,), (1,)), ((), ())), precision=precise, preferred_element_type=jnp.float32)
    squared = left_sq[:, None] + right_sq[None, :] - 2.0 * cross
    scaled = root_five * jnp.sqrt(jnp.maximum(squared, 1.0)) / length_scale
    kernel = (1.0 + scaled + scaled * scaled / 3.0) * jnp.exp(-scaled)
    return kernel + jnp.where(left_ids[:, None] == right_ids[None, :], nugget, 0.0)

def product(left, right):
    return jnp.dot(left.astype(jnp.float32), right.astype(jnp.float32), precision=precise, preferred_element_type=jnp.float32)

def outer_product(left, right):
    return lax.dot_general(left.astype(jnp.float32), right.astype(jnp.float32), (((1,), (1,)), ((), ())), precision=precise, preferred_element_type=jnp.float32)

def to_slab(stored, count):
    width = stored.shape[1]
    return stored.reshape(count, ORDER // (count * NB), NB, width).transpose(1, 0, 2, 3).reshape(ORDER, width)

def to_stored(slab, count):
    width = slab.shape[1]
    return slab.reshape(ORDER // (count * NB), count, NB, width).transpose(1, 0, 2, 3).reshape(ORDER, width)

def reference(archive, slab_index, targets):
    descriptors = jnp.take(archive, slab_index, axis=0)
    positions = jnp.arange(ORDER, dtype=jnp.int32)
    right_side = to_slab(targets, N_COL)
    leading = PANELS * NB
    columns = matern(descriptors, descriptors[:leading], positions, positions[:leading])
    identity = jnp.eye(NB, dtype=jnp.float32)
    panel_list = []
    for step in range(PANELS):
        first = step * NB
        column = columns[:, first:first + NB]
        for earlier in panel_list:
            column = column - outer_product(earlier, earlier[first:first + NB])
        lower = jnp.linalg.cholesky(column[first:first + NB])
        inverse = lax.linalg.triangular_solve(lower, identity, left_side=True, lower=True)
        panel_list.append(outer_product(column, inverse))
    stacked = jnp.concatenate(panel_list, axis=1)

    def kernel_rows(rows):
        return product(matern(jnp.take(descriptors, rows, axis=0), descriptors, rows, positions), right_side)
    whole = lax.map(kernel_rows, positions.reshape(ORDER // NB, NB)).reshape(ORDER, NT)
    result = whole - product(stacked, product(stacked.T, right_side))
    return (to_stored(stacked, N_ROW), to_stored(result, N_ROW))
```

```python
import functools

import jax
import jax.numpy as jnp
from jax import lax
from jax.experimental import pallas as pl
from jax.experimental.pallas import tpu as pltpu
from jax.sharding import PartitionSpec as P

NB = 256
PANELS = 2
BLOCK = 128
GROUP = 4

exact = lax.Precision.HIGHEST
precise = lax.Precision.HIGH
length_scale = 16.0
nugget = 1.0
root_five = 5.0**0.5


def profile_of(squared):
    scaled = (root_five / length_scale) * jnp.sqrt(jnp.maximum(squared, 1.0))
    return (1.0 + scaled + scaled * scaled * (1.0 / 3.0)) * jnp.exp(-scaled)


def matern(left, right, left_ids, right_ids, precision=exact):
    left_sq = jnp.sum(left * left, axis=1)
    right_sq = jnp.sum(right * right, axis=1)
    cross = outer_product(left, right, precision)
    squared = left_sq[:, None] + right_sq[None, :] - 2.0 * cross
    return profile_of(squared) + jnp.where(left_ids[:, None] == right_ids[None, :], nugget, 0.0)


def typical(left, right):
    squares = jnp.sum(left * left) / left.shape[0] + jnp.sum(right * right) / right.shape[0]
    return profile_of(squares - 2.0 * jnp.sum(jnp.mean(left, axis=0) * jnp.mean(right, axis=0)))


def product(left, right, precision=precise):
    return jnp.dot(left, right, precision=precision, preferred_element_type=jnp.float32)


def outer_product(left, right, precision=precise):
    return lax.dot_general(
        left, right, (((1,), (1,)), ((), ())), precision=precision, preferred_element_type=jnp.float32
    )


def eliminate(a_ref, w_ref):
    size = a_ref.shape[0]
    lane = lax.broadcasted_iota(jnp.int32, (size, size), 1)
    row = lax.broadcasted_iota(jnp.int32, (size, size), 0)
    one_lane = lax.broadcasted_iota(jnp.int32, (1, size), 1)
    w_ref[...] = jnp.where(lane == row, 1.0, 0.0)

    def step(index, carry):
        first = index * GROUP
        whole, inverse = a_ref[...], w_ref[...]
        rows = [a_ref[pl.ds(first + t, 1), :] for t in range(GROUP)]
        done = [w_ref[pl.ds(first + t, 1), :] for t in range(GROUP)]
        cols = [
            jnp.sum(jnp.where(lane == first + t, whole, 0.0), axis=1, keepdims=True)
            for t in range(GROUP)
        ]
        spots = [
            [
                jnp.sum(jnp.where(one_lane == first + u, rows[t], 0.0), axis=1, keepdims=True)
                if u >= t
                else None
                for u in range(GROUP)
            ]
            for t in range(GROUP)
        ]
        below = row >= first + GROUP
        for t in range(GROUP):
            pivot = 1.0 / spots[t][t]
            for u in range(t + 1, GROUP):
                ratio = spots[t][u] * pivot
                rows[u] = rows[u] - ratio * rows[t]
                done[u] = done[u] - ratio * done[t]
                cols[u] = cols[u] - ratio * cols[t]
                for v in range(u, GROUP):
                    spots[u][v] = spots[u][v] - ratio * spots[t][v]
            factor = jnp.where(below, cols[t] * pivot, 0.0)
            whole = whole - factor * rows[t]
            inverse = inverse - factor * done[t]
        a_ref[...] = whole
        w_ref[...] = inverse
        for t in range(GROUP):
            w_ref[pl.ds(first + t, 1), :] = done[t] * lax.rsqrt(spots[t][t])
        return carry

    lax.fori_loop(0, size // GROUP, step, 0)


def factor_kernel(descs_ref, out_ref, full, tile, inv):
    leading = descs_ref.shape[0]
    descs = descs_ref[...]
    powers = descs * descs
    left_sq = jnp.sum(powers, axis=1, keepdims=True)
    right_sq = outer_product(jnp.ones((8, descs.shape[1]), jnp.float32), powers, exact)[0:1, :]
    squared = left_sq + right_sq - 2.0 * outer_product(descs, descs, exact)
    row = lax.broadcasted_iota(jnp.int32, (leading, leading), 0)
    col = lax.broadcasted_iota(jnp.int32, (leading, leading), 1)
    full[...] = profile_of(squared) + jnp.where(row == col, nugget, 0.0)
    out_ref[...] = jnp.where(row == col, 1.0, 0.0)
    for start in range(0, leading, BLOCK):
        stop = start + BLOCK
        tile[...] = full[start:stop, start:stop]
        eliminate(tile, inv)
        out_ref[start:stop, :] = product(inv[...], out_ref[start:stop, :], exact)
        if stop < leading:
            lower = outer_product(full[stop:, start:stop], inv[...], exact)
            full[stop:, stop:] = full[stop:, stop:] - outer_product(lower, lower, exact)
            out_ref[stop:, :] = out_ref[stop:, :] - product(lower, out_ref[start:stop, :], exact)


def inverse_factor(descs):
    leading = descs.shape[0]
    return pl.pallas_call(
        factor_kernel,
        out_shape=jax.ShapeDtypeStruct((leading, leading), jnp.float32),
        in_specs=[pl.BlockSpec(memory_space=pltpu.VMEM)],
        out_specs=pl.BlockSpec(memory_space=pltpu.VMEM),
        scratch_shapes=[
            pltpu.VMEM((leading, leading), jnp.float32),
            pltpu.VMEM((BLOCK, BLOCK), jnp.float32),
            pltpu.VMEM((BLOCK, BLOCK), jnp.float32),
        ],
        compiler_params=pltpu.CompilerParams(vmem_limit_bytes=32 * 1024 * 1024),
        cost_estimate=pl.CostEstimate(flops=60_000_000_000, bytes_accessed=2_000_000, transcendentals=300_000),
    )(descs)


def capacity(count, shards):
    mean = count // shards
    return min(count, -(-int(mean + 6.0 * mean**0.5 + 8.0) // 8) * 8)


def ranks(owner, shards):
    count = owner.shape[0]
    width = 128
    hot = (owner[None, :] == jnp.arange(shards, dtype=jnp.int32)[:, None]).astype(jnp.float32)
    hot = hot.reshape(shards, count // width, width)
    ahead = jnp.triu(jnp.ones((width, width), jnp.float32), 1)
    within = lax.dot_general(hot, ahead, (((2,), (0,)), ((), ())), preferred_element_type=jnp.float32)
    blocks = jnp.triu(jnp.ones((count // width, count // width), jnp.float32), 1)
    prior = product(jnp.sum(hot, axis=2), blocks, exact)
    rank = jnp.sum(hot * (within + prior[:, :, None]), axis=0)
    return rank.reshape(count).astype(jnp.int32)


def fetch_compact(archive, wanted, row_place, row_count):
    shard = archive.shape[0]
    cap = capacity(wanted.shape[0], row_count)
    owner = wanted // shard
    rank = ranks(owner, row_count)
    slots = jnp.arange(cap, dtype=jnp.int32)
    hit = (rank[None, :] == slots[:, None]) & (owner == row_place)[None, :]
    mine = jnp.sum(jnp.where(hit, (wanted % shard)[None, :], 0), axis=1)
    block = jnp.take(archive, mine, axis=0, mode="clip")
    gathered = lax.all_gather(block, "row", axis=0, tiled=True)
    return jnp.take(gathered, owner * cap + rank, axis=0, mode="clip")


def fetch_dense(archive, wanted, row_place, row_count):
    shard = archive.shape[0]
    local = wanted - row_place * shard
    inside = (local >= 0) & (local < shard)
    picked = jnp.take(archive, jnp.clip(local, 0, shard - 1), axis=0, mode="clip")
    return lax.psum(jnp.where(inside[:, None], picked, 0.0), "row")


def per_device(archive, slab_index, targets):
    row_count = lax.axis_size("row")
    col_count = lax.axis_size("col")
    row_place = lax.axis_index("row")
    col_place = lax.axis_index("col")
    order = slab_index.shape[0]
    shard = archive.shape[0]
    features = archive.shape[1]
    rows_local = order // row_count
    cols_local = order // col_count
    leading = PANELS * NB
    by_tile = slab_index.reshape(cols_local // NB, col_count, NB)
    col_wanted = lax.dynamic_index_in_dim(by_tile, col_place, 1, keepdims=False).reshape(cols_local)
    lead_wanted = slab_index[:leading]

    shards = jnp.arange(row_count, dtype=jnp.int32)
    col_load = jnp.sum((by_tile // shard)[..., None] == shards, axis=(0, 2))
    lead_load = jnp.sum((lead_wanted // shard)[:, None] == shards, axis=0)
    fits = (jnp.max(col_load) <= capacity(cols_local, row_count)) & (
        jnp.max(lead_load) <= capacity(leading, row_count)
    )

    def collect(fetch, archive, lead_wanted, col_wanted):
        lead = fetch(archive, lead_wanted, row_place, row_count)
        cols = fetch(archive, col_wanted, row_place, row_count)
        return lead, cols, inverse_factor(lead)

    lead_descs, col_descs, inverse = lax.cond(
        fits,
        functools.partial(collect, fetch_compact),
        functools.partial(collect, fetch_dense),
        archive,
        lead_wanted,
        col_wanted,
    )

    ratio = row_count // col_count
    tiles = col_descs.reshape(rows_local // NB, ratio, NB, features)
    row_descs = lax.dynamic_index_in_dim(tiles, row_place // col_count, 1, keepdims=False)
    row_descs = row_descs.reshape(rows_local, features)
    apart = col_place ^ (row_place % col_count)
    bit = col_count // 2
    while bit:
        pairs = []
        for r in range(row_count):
            owner = r % col_count
            for c in range(col_count):
                if (c ^ owner) & (2 * bit - 1) == 0:
                    pairs.append((r * col_count + c, r * col_count + (c ^ bit)))
        came = lax.ppermute(row_descs, ("row", "col"), pairs)
        row_descs = jnp.where((apart & (2 * bit - 1)) == bit, came, row_descs)
        bit //= 2

    def ids(owner, local, count):
        return (local // NB * count + owner) * NB + local % NB

    row_ids = ids(row_place, jnp.arange(rows_local, dtype=jnp.int32), row_count)
    col_ids = ids(col_place, jnp.arange(cols_local, dtype=jnp.int32), col_count)
    lead_ids = jnp.arange(leading, dtype=jnp.int32)

    lead_rows = product(matern(lead_descs, col_descs, lead_ids, col_ids), targets, exact)
    reduced = product(inverse, lead_rows, exact)
    stacked = outer_product(matern(row_descs, lead_descs, row_ids, lead_ids), inverse, exact)
    slab = matern(row_descs, col_descs, row_ids, col_ids, precise)
    center = typical(row_descs, col_descs)
    part = product(slab - center, targets) + center * jnp.sum(targets, axis=0)[None, :]
    part = part - product(stacked, reduced, exact)
    result = lax.psum_scatter(part, "col", scatter_dimension=0, tiled=True)
    return (stacked, result)


def solution(mesh):
    placed = (P("row", None), P(), P("col", None))
    return jax.shard_map(
        per_device,
        mesh=mesh,
        in_specs=placed,
        out_specs=(P("row", None), P(("row", "col"), None)),
        check_vma=False,
    )
```

```python
import functools

import jax
import jax.numpy as jnp
from jax import lax
from jax.experimental import pallas as pl
from jax.experimental.pallas import tpu as pltpu
from jax.sharding import PartitionSpec as P

NB = 256
PANELS = 2
BLOCK = 128
GROUP = 4
CHUNKS = 2

exact = lax.Precision.HIGHEST
precise = lax.Precision.HIGH
length_scale = 16.0
nugget = 1.0
root_five = 5.0**0.5


def profile_of(squared):
    scaled = (root_five / length_scale) * jnp.sqrt(jnp.maximum(squared, 1.0))
    return (1.0 + scaled + scaled * scaled * (1.0 / 3.0)) * jnp.exp(-scaled)


def matern(left, right, left_ids, right_ids, precision=exact):
    left_sq = jnp.sum(left * left, axis=1)
    right_sq = jnp.sum(right * right, axis=1)
    cross = outer_product(left, right, precision)
    squared = left_sq[:, None] + right_sq[None, :] - 2.0 * cross
    return profile_of(squared) + jnp.where(left_ids[:, None] == right_ids[None, :], nugget, 0.0)


def typical(left, right):
    squares = jnp.sum(left * left) / left.shape[0] + jnp.sum(right * right) / right.shape[0]
    return profile_of(squares - 2.0 * jnp.sum(jnp.mean(left, axis=0) * jnp.mean(right, axis=0)))


def product(left, right, precision=precise):
    return jnp.dot(left, right, precision=precision, preferred_element_type=jnp.float32)


def outer_product(left, right, precision=precise):
    return lax.dot_general(
        left, right, (((1,), (1,)), ((), ())), precision=precision, preferred_element_type=jnp.float32
    )


def split(value):
    high = lax.reduce_precision(value, 8, 7)
    return high.astype(jnp.bfloat16), (value - high).astype(jnp.bfloat16)


def product_split(left, right_parts):
    high, low = split(left)
    right_high, right_low = right_parts

    def dot(a, b):
        return jnp.dot(a, b, preferred_element_type=jnp.float32)

    return dot(high, right_high) + (dot(high, right_low) + dot(low, right_high))


def eliminate(a_ref, w_ref):
    size = a_ref.shape[0]
    lane = lax.broadcasted_iota(jnp.int32, (size, size), 1)
    row = lax.broadcasted_iota(jnp.int32, (size, size), 0)
    one_lane = lax.broadcasted_iota(jnp.int32, (1, size), 1)
    w_ref[...] = jnp.where(lane == row, 1.0, 0.0)

    def step(index, carry):
        first = index * GROUP
        whole, inverse = a_ref[...], w_ref[...]
        rows = [a_ref[pl.ds(first + t, 1), :] for t in range(GROUP)]
        done = [w_ref[pl.ds(first + t, 1), :] for t in range(GROUP)]
        cols = [
            jnp.sum(jnp.where(lane == first + t, whole, 0.0), axis=1, keepdims=True)
            for t in range(GROUP)
        ]
        spots = [
            [
                jnp.sum(jnp.where(one_lane == first + u, rows[t], 0.0), axis=1, keepdims=True)
                if u >= t
                else None
                for u in range(GROUP)
            ]
            for t in range(GROUP)
        ]
        below = row >= first + GROUP
        for t in range(GROUP):
            pivot = 1.0 / spots[t][t]
            for u in range(t + 1, GROUP):
                ratio = spots[t][u] * pivot
                rows[u] = rows[u] - ratio * rows[t]
                done[u] = done[u] - ratio * done[t]
                cols[u] = cols[u] - ratio * cols[t]
                for v in range(u, GROUP):
                    spots[u][v] = spots[u][v] - ratio * spots[t][v]
            factor = jnp.where(below, cols[t] * pivot, 0.0)
            whole = whole - factor * rows[t]
            inverse = inverse - factor * done[t]
        a_ref[...] = whole
        w_ref[...] = inverse
        for t in range(GROUP):
            w_ref[pl.ds(first + t, 1), :] = done[t] * lax.rsqrt(spots[t][t])
        return carry

    lax.fori_loop(0, size // GROUP, step, 0)


def factor_kernel(descs_ref, out_ref, full, tile, inv):
    leading = descs_ref.shape[0]
    descs = descs_ref[...]
    powers = descs * descs
    left_sq = jnp.sum(powers, axis=1, keepdims=True)
    right_sq = outer_product(jnp.ones((8, descs.shape[1]), jnp.float32), powers, exact)[0:1, :]
    squared = left_sq + right_sq - 2.0 * outer_product(descs, descs, exact)
    row = lax.broadcasted_iota(jnp.int32, (leading, leading), 0)
    col = lax.broadcasted_iota(jnp.int32, (leading, leading), 1)
    full[...] = profile_of(squared) + jnp.where(row == col, nugget, 0.0)
    out_ref[...] = jnp.where(row == col, 1.0, 0.0)
    for start in range(0, leading, BLOCK):
        stop = start + BLOCK
        tile[...] = full[start:stop, start:stop]
        eliminate(tile, inv)
        out_ref[start:stop, :] = product(inv[...], out_ref[start:stop, :], exact)
        if stop < leading:
            lower = outer_product(full[stop:, start:stop], inv[...], exact)
            full[stop:, stop:] = full[stop:, stop:] - outer_product(lower, lower, exact)
            out_ref[stop:, :] = out_ref[stop:, :] - product(lower, out_ref[start:stop, :], exact)


def inverse_factor(descs):
    leading = descs.shape[0]
    return pl.pallas_call(
        factor_kernel,
        out_shape=jax.ShapeDtypeStruct((leading, leading), jnp.float32),
        in_specs=[pl.BlockSpec(memory_space=pltpu.VMEM)],
        out_specs=pl.BlockSpec(memory_space=pltpu.VMEM),
        scratch_shapes=[
            pltpu.VMEM((leading, leading), jnp.float32),
            pltpu.VMEM((BLOCK, BLOCK), jnp.float32),
            pltpu.VMEM((BLOCK, BLOCK), jnp.float32),
        ],
        compiler_params=pltpu.CompilerParams(vmem_limit_bytes=32 * 1024 * 1024),
        cost_estimate=pl.CostEstimate(flops=60_000_000_000, bytes_accessed=2_000_000, transcendentals=300_000),
    )(descs)


def capacity(count, shards):
    mean = count // shards
    return min(count, -(-int(mean + 4.1 * mean**0.5) // 8) * 8)


def ranks(owner, shards):
    count = owner.shape[0]
    width = 128
    hot = (owner[None, :] == jnp.arange(shards, dtype=jnp.int32)[:, None]).astype(jnp.float32)
    hot = hot.reshape(shards, count // width, width)
    ahead = jnp.triu(jnp.ones((width, width), jnp.float32), 1)
    within = lax.dot_general(hot, ahead, (((2,), (0,)), ((), ())), preferred_element_type=jnp.float32)
    blocks = jnp.triu(jnp.ones((count // width, count // width), jnp.float32), 1)
    prior = product(jnp.sum(hot, axis=2), blocks, exact)
    rank = jnp.sum(hot * (within + prior[:, :, None]), axis=0)
    return rank.reshape(count).astype(jnp.int32)


def pick_kernel(spots_ref, source_ref, out_ref):
    count = out_ref.shape[0]
    base = pl.program_id(0) * count
    unroll = 16

    def step(index, carry):
        for t in range(unroll):
            place = index * unroll + t
            out_ref[pl.ds(place, 1), :] = source_ref[pl.ds(spots_ref[base + place], 1), :]
        return carry

    lax.fori_loop(0, count // unroll, step, 0)


def pick_rows(source, spots):
    count, width = spots.shape[0], source.shape[1]
    block = NB
    return pl.pallas_call(
        pick_kernel,
        grid_spec=pltpu.PrefetchScalarGridSpec(
            num_scalar_prefetch=1,
            grid=(count // block,),
            in_specs=[pl.BlockSpec(source.shape, lambda i, spots: (0, 0))],
            out_specs=pl.BlockSpec((block, width), lambda i, spots: (i, 0)),
        ),
        out_shape=jax.ShapeDtypeStruct((count, width), jnp.float32),
        compiler_params=pltpu.CompilerParams(vmem_limit_bytes=32 * 1024 * 1024),
    )(spots, source)


def fetch_compact(archive, wanted, row_place, row_count):
    shard = archive.shape[0]
    cap = capacity(wanted.shape[0], row_count)
    owner = wanted // shard
    rank = ranks(owner, row_count)
    slots = jnp.arange(cap, dtype=jnp.int32)
    hit = (rank[None, :] == slots[:, None]) & (owner == row_place)[None, :]
    mine = jnp.sum(jnp.where(hit, (wanted % shard)[None, :], 0), axis=1)
    block = jnp.take(archive, mine, axis=0, mode="clip")
    gathered = lax.all_gather(block, "row", axis=0, tiled=True)
    return pick_rows(gathered, jnp.minimum(owner * cap + rank, gathered.shape[0] - 1))


def fetch_dense(archive, wanted, row_place, row_count):
    shard = archive.shape[0]
    local = wanted - row_place * shard
    inside = (local >= 0) & (local < shard)
    picked = jnp.take(archive, jnp.clip(local, 0, shard - 1), axis=0, mode="clip")
    return lax.psum(jnp.where(inside[:, None], picked, 0.0), "row")


def per_device(archive, slab_index, targets):
    row_count = lax.axis_size("row")
    col_count = lax.axis_size("col")
    row_place = lax.axis_index("row")
    col_place = lax.axis_index("col")
    order = slab_index.shape[0]
    shard = archive.shape[0]
    features = archive.shape[1]
    rows_local = order // row_count
    cols_local = order // col_count
    leading = PANELS * NB
    by_tile = slab_index.reshape(cols_local // NB, col_count, NB)
    col_wanted = lax.dynamic_index_in_dim(by_tile, col_place, 1, keepdims=False).reshape(cols_local)
    lead_wanted = slab_index[:leading]

    shards = jnp.arange(row_count, dtype=jnp.int32)
    col_load = jnp.sum((by_tile // shard)[..., None] == shards, axis=(0, 2))
    lead_load = jnp.sum((lead_wanted // shard)[:, None] == shards, axis=0)
    fits = (jnp.max(col_load) <= capacity(cols_local, row_count)) & (
        jnp.max(lead_load) <= capacity(leading, row_count)
    )

    def collect(fetch, archive, lead_wanted, col_wanted):
        lead = fetch(archive, lead_wanted, row_place, row_count)
        cols = fetch(archive, col_wanted, row_place, row_count)
        return lead, cols, inverse_factor(lead)

    lead_descs, col_descs, inverse = lax.cond(
        fits,
        functools.partial(collect, fetch_compact),
        functools.partial(collect, fetch_dense),
        archive,
        lead_wanted,
        col_wanted,
    )

    ratio = row_count // col_count
    tiles = col_descs.reshape(rows_local // NB, ratio, NB, features)
    row_descs = lax.dynamic_index_in_dim(tiles, row_place // col_count, 1, keepdims=False)
    row_descs = row_descs.reshape(rows_local, features)
    apart = col_place ^ (row_place % col_count)
    bit = col_count // 2
    while bit:
        pairs = []
        for r in range(row_count):
            owner = r % col_count
            for c in range(col_count):
                if (c ^ owner) & (2 * bit - 1) == 0:
                    pairs.append((r * col_count + c, r * col_count + (c ^ bit)))
        came = lax.ppermute(row_descs, ("row", "col"), pairs)
        row_descs = jnp.where((apart & (2 * bit - 1)) == bit, came, row_descs)
        bit //= 2

    def ids(owner, local, count):
        return (local // NB * count + owner) * NB + local % NB

    row_ids = ids(row_place, jnp.arange(rows_local, dtype=jnp.int32), row_count)
    col_ids = ids(col_place, jnp.arange(cols_local, dtype=jnp.int32), col_count)
    lead_ids = jnp.arange(leading, dtype=jnp.int32)

    target_parts = split(targets)
    target_sum = jnp.sum(targets, axis=0)[None, :]

    def times_targets(descs, own_ids, precision):
        center = typical(descs, col_descs)
        kernel = matern(descs, col_descs, own_ids, col_ids, precision)
        return product_split(kernel - center, target_parts) + center * target_sum

    lead_rows = times_targets(lead_descs, lead_ids, precise)
    reduced = product(inverse, lead_rows, exact)
    stacked = outer_product(matern(row_descs, lead_descs, row_ids, lead_ids), inverse, exact)
    removed = product(stacked, reduced, exact)

    def chunk(array, index):
        pieces = array.reshape((col_count, CHUNKS, -1) + array.shape[1:])
        return pieces[:, index].reshape((-1,) + array.shape[1:])

    results = []
    for index in range(CHUNKS):
        part = times_targets(chunk(row_descs, index), chunk(row_ids, index), precise)
        part = part - chunk(removed, index)
        results.append(lax.psum_scatter(part, "col", scatter_dimension=0, tiled=True))
    result = jnp.concatenate(results, axis=0)
    return (stacked, result)


def solution(mesh):
    placed = (P("row", None), P(), P("col", None))
    return jax.shard_map(
        per_device,
        mesh=mesh,
        in_specs=placed,
        out_specs=(P("row", None), P(("row", "col"), None)),
        check_vma=False,
    )
```
